32 devices in a mesh: job: 2 (over x), dp: 2 (over core), mp: 8 (over z, y).
Axes of the slice: x: 2, y: 2, z: 4, core: 2. Of those that a mesh axis runs over, the one named last changes fastest.
Arguments:
- output_gradient: bfloat16 [8192, 5120], P(('job', 'dp', 'mp')), parts along dimension 0, may hold values from -6 to 6
- hidden: bfloat16 [8192, 12800], P(('job', 'dp'), 'mp'), parts along dimension 0, may hold values from -6 to 6
- down_weight_frozen: bfloat16 [12800, 5120], P('mp'), may hold values from -0.0546875 to 0.0546875
- adapter_down_maps: bfloat16 [16, 12800, 16], P(None, 'mp'), may hold values from -0.14941406 to 0.14941406
- adapter_up_maps: bfloat16 [16, 16, 5120], P(None, None, 'mp'), may hold values from -0.078125 to 0.078125
- segment_length_list: int32 [4, 16], P(('job', 'dp')), parts along dimension 0, may hold values from 1 to 512, 2048 in all within a row
- segment_adapter_index: int32 [4, 16], P(('job', 'dp')), parts along dimension 0, may hold values from 0 to 15
- owner_slot_adapter: int32 [32], P('job'), parts along dimension 0, may hold values from 0 to 15, as said below
- adapter_token_totals: int32 [32], P('job'), parts along dimension 0, may hold values from 64 to 1023
Outputs:
- grad_hidden: bfloat16 [8192, 12800], P(('job', 'dp'), 'mp'), parts along dimension 0
- grad_a: float32 [32, 12800, 16], P(('job', 'dp'), 'mp'), parts along dimension 0
- grad_b: float32 [32, 16, 5120], P(('job', 'dp'), None, 'mp'), parts along dimension 0
The draws below stay inside these ranges and needn't reach their ends.
There are 2 independent parts, one for each index of `job`. The reference program is written for one: setup_inputs(seed, part) draws one part's arguments, and reference() takes and returns one part's arrays. A program takes and returns all parts, laid end to end along the dimension named above; an argument that names none is the same for every part. Nothing has to cross between parts.
Inputs may be any that keep to these rules, and one draw needn't show every extreme that they name: `segment_length_list`: in each data group the lengths sum to 2048; the largest is exactly 512. `owner_slot_adapter`: each adapter stands in exactly one slot.
All inputs are finite; a program needn't handle non-finite values.
Results may differ from the reference program's by a relative error of at most 0.0055.
Values may be sent and summed in bfloat16 or wider, within the bound.
A program may use at most 192 MiB of HBM per device.

```python
import math
import jax
import jax.numpy as jnp
import numpy as np
from jax import lax

MODEL_WIDTH = 5120
HIDDEN_UNITS = 12800
ADAPTER_RANK = 16
ADAPTER_COUNT = 16
TOK = 2048
SEGS = 16
MOST_SEG = 512
TOKENS = 4096
N_DP = 2


def draw_owner_slot_adapter(key, part):
    key = jax.random.fold_in(key, 7)
    return jax.random.permutation(key, jnp.arange(ADAPTER_COUNT, dtype=jnp.int32)).astype(jnp.int32)


def plant(drawn, stream_key, smallest, top_value):
    extent = drawn.shape
    place = [jax.random.randint(jax.random.fold_in(stream_key, axis), (), 0, extent[axis]) for axis in range(len(extent))]
    drawn = drawn.at[tuple(place)].set(smallest)
    longest = extent.index(max(extent))
    place[longest] = (place[longest] + 1) % extent[longest]
    return drawn.at[tuple(place)].set(top_value)


def levels(own_key, extent, split, low, largest):
    def one(axis_at, blocks):
        steps = jax.random.uniform(jax.random.fold_in(jax.random.fold_in(own_key, 6), axis_at), (blocks,), jnp.float32, low / len(split), largest / len(split))
        return jnp.repeat(jnp.exp(steps), extent[axis_at] // blocks).reshape((-1,) + (1,) * (len(extent) - axis_at - 1))

    gain = one(*split[0])
    for cut in split[1:]:
        gain = gain * one(*cut)
    return gain


def rank_table(amount, lean):
    loads = [(1 << 20) // math.isqrt(grade ** lean) + 1 for grade in range(1, amount + 1)]
    deviation = 1 + sum(loads) // (1 << 30)
    return np.cumsum(np.array([max(1, weight // deviation) for weight in loads]))


def ranked_ids(rng, shape, number_of, skew):
    table = rank_table(number_of, skew)
    pick = jax.random.randint(jax.random.fold_in(rng, 1), shape, 0, int(table[number_of - 1]))
    rank = jnp.searchsorted(jnp.asarray(table, jnp.int32), pick, side="right")
    return jax.random.permutation(jax.random.fold_in(rng, 2), number_of)[rank].astype(jnp.int32)


def length_profile(number_of, total, bound, skew):
    portions = [(1 << 20) // math.isqrt(standing ** skew) + 1 for standing in range(2, number_of + 1)]
    surplus, given = total - bound - (number_of - 1), [1] * (number_of - 1)
    while surplus > 0:
        candidates = [i for i in range(number_of - 1) if given[i] < bound]
        mass, remaining = sum([portions[i] for i in candidates]), surplus
        for i in candidates:
            more = min(bound - given[i], max(1, remaining * portions[i] // mass), surplus)
            given[i] = given[i] + more
            surplus = surplus - more
    return np.array([bound] + given)


def ragged(rng, number_of, total, most, slope):
    if number_of == 2:
        one = jax.random.randint(rng, (), max(1, total - most), min(most, total - 1) + 1)
        return jnp.stack([one, total - one])
    sizes = jnp.asarray(length_profile(number_of, total, most, slope), jnp.int32)
    couples = (number_of - 1) // 2
    source_of, receiver = sizes[1:1 + 2 * couples:2], sizes[2:2 + 2 * couples:2]
    room = jnp.minimum(source_of - 1, most - receiver)
    shifted = jax.random.randint(jax.random.fold_in(rng, 1), (couples,), 0, 1 << 20) % (room + 1)
    sizes = sizes.at[1:1 + 2 * couples:2].set(source_of - shifted).at[2:2 + 2 * couples:2].set(receiver + shifted)
    return sizes[jax.random.permutation(jax.random.fold_in(rng, 2), number_of)]


def centred(key, extent, deviation, bound, split=(), kind=jnp.bfloat16):
    factor_of = levels(key, extent, split, -0.22, 0.18) if split else 1.0
    result = jax.random.normal(key, extent, jnp.float32) * deviation * factor_of
    return jnp.minimum(jnp.maximum(result, -bound), bound).astype(kind)


def setup_inputs(seed: int = 0, part: int = 0) -> dict:
    seeds = jax.random.split(jax.random.key(seed), 10)
    part_keys = jax.random.split(jax.random.fold_in(seeds[9], part), 10)
    return {
        "output_gradient": centred(part_keys[0], (TOKENS, MODEL_WIDTH), 1.0, 6.0, ((0, 16),)),
        "hidden": centred(part_keys[1], (TOKENS, HIDDEN_UNITS), 1.0, 6.0, ((0, 2), (1, 8))),
        "down_weight_frozen": centred(seeds[2], (HIDDEN_UNITS, MODEL_WIDTH), HIDDEN_UNITS ** -0.5, 0.0546875, ((0, 8),)),
        "adapter_down_maps": centred(seeds[3], (ADAPTER_COUNT, HIDDEN_UNITS, ADAPTER_RANK), 0.025, 0.14941406, ((1, 8),)),
        "adapter_up_maps": centred(seeds[4], (ADAPTER_COUNT, ADAPTER_RANK, MODEL_WIDTH), MODEL_WIDTH ** -0.5, 0.078125, ((2, 8),)),
        "segment_length_list": jax.vmap(lambda own: ragged(own, SEGS, TOK, MOST_SEG, 2))(jax.random.split(part_keys[5], N_DP)).reshape((N_DP, SEGS)).astype(jnp.int32),
        "segment_adapter_index": plant(ranked_ids(part_keys[6], (N_DP, SEGS), ADAPTER_COUNT, 2), jax.random.fold_in(part_keys[6], 3), 0, ADAPTER_COUNT - 1).astype(jnp.int32),
        "owner_slot_adapter": draw_owner_slot_adapter(jax.random.fold_in(jax.random.fold_in(seeds[9], part), 71), part),
        "adapter_token_totals": plant(jax.random.randint(part_keys[8], (ADAPTER_COUNT,), 64, 1024), jax.random.fold_in(part_keys[8], 1), 64, 1023).astype(jnp.int32),
    }


def adapter_table(lengths, labels, count_tok, adapter_token_count):
    ends = jnp.cumsum(lengths).astype(jnp.int32)
    starts = ends - lengths
    position = jnp.arange(count_tok, dtype=jnp.int32)[:, None]
    inside = ((position >= starts[None, :]) & (position < ends[None, :])).astype(jnp.float32)
    label_hot = (labels[:, None] == jnp.arange(adapter_token_count, dtype=jnp.int32)[None, :]).astype(jnp.float32)
    return jnp.dot(inside, label_hot, precision=lax.Precision.HIGHEST)


def masked(values, owner, adapter_rank_size):
    shaped = values.reshape(values.shape[0], owner.shape[1], adapter_rank_size)
    return jnp.sum(shaped * owner[:, :, None], axis=1)


def spread(vector, owner):
    return (owner.astype(jnp.bfloat16)[:, :, None] * vector[:, None, :]).reshape(vector.shape[0], -1)


def reference(output_gradient, hidden, down_weight_frozen, adapter_down_maps, adapter_up_maps, segment_length_list, segment_adapter_index, owner_slot_adapter, adapter_token_totals):
    flattened_down_maps = jnp.transpose(adapter_down_maps, (1, 0, 2)).reshape(HIDDEN_UNITS, ADAPTER_COUNT * ADAPTER_RANK)
    flattened_up_maps = adapter_up_maps.reshape(ADAPTER_COUNT * ADAPTER_RANK, MODEL_WIDTH)
    raw_a = jnp.zeros((HIDDEN_UNITS, ADAPTER_COUNT * ADAPTER_RANK), jnp.float32)
    raw_b = jnp.zeros((ADAPTER_COUNT * ADAPTER_RANK, MODEL_WIDTH), jnp.float32)
    pieces = []
    for group in range(N_DP):
        rows_dy = output_gradient[group * TOK:(group + 1) * TOK]
        rows_h = hidden[group * TOK:(group + 1) * TOK]
        owner = adapter_table(segment_length_list[group], segment_adapter_index[group], TOK, ADAPTER_COUNT)
        low_up = masked(jnp.dot(rows_dy, flattened_up_maps.T, preferred_element_type=jnp.float32), owner, ADAPTER_RANK).astype(jnp.bfloat16)
        low_down = masked(jnp.dot(rows_h, flattened_down_maps, preferred_element_type=jnp.float32), owner, ADAPTER_RANK).astype(jnp.bfloat16)
        up_spread = spread(low_up, owner)
        down_spread = spread(low_down, owner)
        main = jnp.dot(rows_dy, down_weight_frozen.T, preferred_element_type=jnp.float32)
        extra = jnp.dot(up_spread, flattened_down_maps.T, preferred_element_type=jnp.float32)
        pieces.append((main + 2.0 * extra).astype(jnp.bfloat16))
        raw_a = raw_a + 2.0 * jnp.dot(rows_h.T, up_spread, preferred_element_type=jnp.float32)
        raw_b = raw_b + 2.0 * jnp.dot(down_spread.T, rows_dy, preferred_element_type=jnp.float32)
    grad_hidden = jnp.concatenate(pieces, axis=0)
    raw_a = jnp.transpose(raw_a.reshape(HIDDEN_UNITS, ADAPTER_COUNT, ADAPTER_RANK), (1, 0, 2))
    raw_b = raw_b.reshape(ADAPTER_COUNT, ADAPTER_RANK, MODEL_WIDTH)
    divisor = adapter_token_totals[owner_slot_adapter].astype(jnp.float32)
    grad_a = raw_a[owner_slot_adapter] / divisor[:, None, None]
    grad_b = raw_b[owner_slot_adapter] / divisor[:, None, None]
    return grad_hidden, grad_a, grad_b
```

```python
import functools

import jax
import jax.numpy as jnp
from jax import lax
from jax.experimental import pallas as pl
from jax.experimental.pallas import tpu as pltpu
from jax.sharding import PartitionSpec as P

MESH = pl.DeviceIdType.MESH
NT = (((1,), (1,)), ((), ()))


def adapter_table(lengths, labels, count_tok, adapter_token_count):
    ends = jnp.cumsum(lengths)
    starts = ends - lengths
    position = jnp.arange(count_tok, dtype=jnp.int32)[:, None]
    inside = ((position >= starts[None, :]) & (position < ends[None, :])).astype(jnp.float32)
    label_hot = (
        labels[:, None] == jnp.arange(adapter_token_count, dtype=jnp.int32)[None, :]
    ).astype(jnp.float32)
    return jnp.dot(inside, label_hot, precision=lax.Precision.HIGHEST)


def chunks_of(rows):
    units = rows // 16
    first = max(1, units // 8)
    rest = units - first
    parts = min(3, rest)
    sizes = [first] + [rest // parts + (1 if i < rest % parts else 0) for i in range(parts)]
    out, at = [], 0
    for size in sizes:
        out.append((at * 16, size * 16))
        at += size
    return out


def gather_kernel(
    n, rank,
    dy_ref, w_ref, ups_ref, down_ref, ids_ref, part_ref,
    gh_ref, spread_ref, low_ref, cols_ref,
    g, w_v, u, out_v, spread_v, land, low_v,
    s_up, s_dn, s_y, s_recv, s_us, s_ur, s_xs, s_xr, s_ps, s_pr, s_ls, s_lr, s_loc, s_out, s_cols,
):
    m = lax.axis_index("mp")
    h = lax.axis_index("dp")
    zs = n // 2
    z, y = m // 2, m % 2
    rows = dy_ref.shape[0]
    half = u.shape[1] // 2
    width = u.shape[2]
    units = w_v.shape[0]
    chunks = chunks_of(rows)
    up, dn, across = m + 2, m - 2, z * 2 + (1 - y)

    load_dy = pltpu.make_async_copy(
        dy_ref, g.at[pl.ds(pl.multiple_of(m * rows, 16), rows)], s_loc.at[0]
    )
    load_w = pltpu.make_async_copy(w_ref, w_v, s_loc.at[1])
    load_u = pltpu.make_async_copy(ups_ref, u.at[m], s_loc.at[2])
    load_dy.start()
    load_u.start()
    load_w.start()

    barrier = pltpu.get_barrier_semaphore()
    for k in range(1, n):
        pl.semaphore_signal(barrier, inc=1, device_id={"mp": lax.rem(m + k, n)}, device_id_type=MESH)
    pl.semaphore_signal(barrier, inc=1, device_id={"dp": 1 - h}, device_id_type=MESH)
    pl.semaphore_wait(barrier, n)

    def block_copy(b, c, sem, to):
        r0, size = chunks[c]
        at = g.at[pl.ds(pl.multiple_of(b * rows + r0, 16), size)]
        return pltpu.make_async_remote_copy(
            src_ref=at, dst_ref=at, send_sem=sem.at[b, c], recv_sem=s_recv.at[b, c],
            device_id={"mp": to}, device_id_type=MESH,
        )

    my_half = pl.ds(pl.multiple_of(h * half, 16), half)
    his_half = pl.ds(pl.multiple_of((1 - h) * half, 16), half)

    def up_copy(k):
        at = u.at[m, my_half]
        return pltpu.make_async_remote_copy(
            src_ref=at, dst_ref=at, send_sem=s_us.at[k], recv_sem=s_ur.at[k],
            device_id={"mp": lax.rem(m + k, n)}, device_id_type=MESH,
        )

    def up_landed(k):
        at = u.at[lax.rem(m + n - k, n), my_half]
        return pltpu.make_async_remote_copy(
            src_ref=at, dst_ref=at, send_sem=s_us.at[k], recv_sem=s_ur.at[k],
            device_id={"mp": lax.rem(m + k, n)}, device_id_type=MESH,
        )

    def up_pass(k, part):
        at = u.at[lax.rem(m + n - k, n), part]
        return pltpu.make_async_remote_copy(
            src_ref=at, dst_ref=at, send_sem=s_xs.at[k], recv_sem=s_xr.at[k],
            device_id={"dp": 1 - h}, device_id_type=MESH,
        )

    def part_copy(k):
        to = lax.rem(m + k, n)
        return pltpu.make_async_remote_copy(
            src_ref=part_ref.at[to], dst_ref=land.at[k], send_sem=s_ps.at[k], recv_sem=s_pr.at[k],
            device_id={"mp": to}, device_id_type=MESH,
        )

    def low_copy(k, b):
        to = lax.rem(m + k, n)
        return pltpu.make_async_remote_copy(
            src_ref=low_v.at[b], dst_ref=low_v.at[b], send_sem=s_ls.at[k], recv_sem=s_lr.at[k],
            device_id={"mp": to}, device_id_type=MESH,
        )

    def start_along(b, c, up_too, dn_too):
        @pl.when(up_too)
        def _():
            block_copy(b, c, s_up, up).start()

        @pl.when(dn_too)
        def _():
            block_copy(b, c, s_dn, dn).start()

    can_up, can_dn = z < zs - 1, z > 0
    load_u.wait()
    for k in range(1, n):
        up_copy(k).start()
    load_dy.wait()
    for c in range(len(chunks)):
        block_copy(m, c, s_y, across).start()
        start_along(m, c, can_up, can_dn)
    for k in range(1, n):
        part_copy(k).start()

    block_copy(across, 0, s_y, across).wait_recv()
    start_along(across, 0, can_up, can_dn)
    for k in range(1, n):
        up_landed(k).wait_recv()
        up_pass(k, my_half).start()
    total = part_ref[m]
    for k in range(1, n):
        part_copy(k).wait_recv()
        total = total + land[k]
    low_v[m] = total.astype(jnp.bfloat16)
    for k in range(1, n):
        low_copy(k, m).start()
    for k in range(1, n):
        up_pass(k, his_half).wait_recv()
    load_w.wait()

    def cols_copy(b):
        r = pl.ds(pl.multiple_of(b * rows, 16), rows)
        if cols_ref.shape[1] == g.shape[1]:
            return pltpu.make_async_copy(g.at[r], cols_ref.at[r], s_cols.at[b])
        c = pl.ds(pl.multiple_of(m * width, 128), width)
        return pltpu.make_async_copy(g.at[r, c], cols_ref.at[r], s_cols.at[b])

    def out_copy(b):
        r = pl.ds(pl.multiple_of(b * rows, 16), rows)
        return pltpu.make_async_copy(out_v.at[r], gh_ref.at[r], s_out.at[b])

    tile = 512
    edges = [(i, min(tile, units - i)) for i in range(0, units, tile)]

    def compute(b):
        r = pl.ds(pl.multiple_of(b * rows, 16), rows)
        cols_copy(b).start()
        val = jnp.zeros((rows, 2 * half), jnp.float32)
        for j in range(n):
            val = val + lax.dot_general(
                g[r, j * width:(j + 1) * width], u[j], NT, preferred_element_type=jnp.float32
            )
        lane = lax.broadcasted_iota(jnp.int32, (rows, 2 * half), 1) // rank
        low = jnp.where(lane == ids_ref[r], val, 0.0).astype(jnp.bfloat16)
        spread_v[r] = low
        for c0, size in edges:
            acc = lax.dot_general(
                g[r], w_v[c0:c0 + size], NT, preferred_element_type=jnp.float32
            )
            acc = acc + 2.0 * lax.dot_general(
                low, down_ref[c0:c0 + size], NT, preferred_element_type=jnp.float32
            )
            out_v[r, c0:c0 + size] = acc.astype(jnp.bfloat16)
        out_copy(b).start()

    def step(d, carry):
        lo, hi = z - d, z + d
        moving = d > 0
        lo_in, hi_in = moving & (lo >= 0), moving & (hi < zs)

        def pass_on(c, side, crosses):
            @pl.when(lo_in)
            def _():
                b = lo * 2 + side
                block_copy(b, c, s_up, across).wait_recv()
                if crosses:
                    block_copy(b, c, s_y, across).start()

                @pl.when(can_up)
                def _():
                    block_copy(b, c, s_up, up).start()

            @pl.when(hi_in)
            def _():
                b = hi * 2 + side
                block_copy(b, c, s_dn, across).wait_recv()
                if crosses:
                    block_copy(b, c, s_y, across).start()

                @pl.when(can_dn)
                def _():
                    block_copy(b, c, s_dn, dn).start()

        for c in range(1, len(chunks)):
            pass_on(c, y, True)
        pass_on(0, y, False)
        pass_on(0, 1 - y, False)

        e = d - 1

        def four(i, carry):
            lower = (i % 2) == 0
            own = i < 2
            dist = jnp.where(own, d, e)
            zz = jnp.where(lower, z - dist, z + dist)
            ok = (dist >= 0) & (zz >= 0) & (zz < zs) & (lower | (dist > 0))
            b = zz * 2 + jnp.where(own, y, 1 - y)

            @pl.when(ok)
            def _():
                @pl.when(jnp.logical_not(own))
                def _():
                    for c in range(1, len(chunks)):
                        block_copy(b, c, s_y, across).wait_recv()
                compute(b)
            return carry

        lax.fori_loop(0, 4, four, 0)
        return carry

    lax.fori_loop(0, zs + 1, step, 0)

    for k in range(1, n):
        low_copy(k, lax.rem(m + n - k, n)).wait_recv()
    low_out = pltpu.make_async_copy(low_v, low_ref, s_loc.at[0])
    spread_out = pltpu.make_async_copy(spread_v, spread_ref, s_loc.at[1])
    low_out.start()
    spread_out.start()

    for k in range(1, n):
        up_copy(k).wait_send()
        up_pass(k, my_half).wait_send()
        part_copy(k).wait_send()
        low_copy(k, m).wait_send()

    def drain(b, carry):
        bz, by = b // 2, b % 2
        for c in range(len(chunks)):
            zway = (by == y) if c else (bz >= 0)

            @pl.when(can_up & (bz <= z) & zway)
            def _():
                block_copy(b, c, s_up, up).wait_send()

            @pl.when(can_dn & (bz >= z) & zway)
            def _():
                block_copy(b, c, s_dn, dn).wait_send()

            @pl.when((by == y) & (True if c else (bz == z)))
            def _():
                block_copy(b, c, s_y, across).wait_send()
        cols_copy(b).wait()
        out_copy(b).wait()
        return carry

    lax.fori_loop(0, n, drain, 0)
    low_out.wait()
    spread_out.wait()


def gather_and_multiply(n, rank, dy, w, ups, down, ids, part):
    rows, model = dy.shape
    units = w.shape[0]
    pairs, width = ups.shape
    whole = n * rows
    cols = width if width % 128 == 0 else model
    count = len(chunks_of(rows))
    any_spec = pl.BlockSpec(memory_space=pl.ANY)
    vmem = pl.BlockSpec(memory_space=pltpu.VMEM)
    dma = pltpu.SemaphoreType.DMA
    return pl.pallas_call(
        functools.partial(gather_kernel, n, rank),
        out_shape=(
            jax.ShapeDtypeStruct((whole, units), jnp.bfloat16),
            jax.ShapeDtypeStruct((whole, pairs), jnp.bfloat16),
            jax.ShapeDtypeStruct((n, rank, rows), jnp.bfloat16),
            jax.ShapeDtypeStruct((whole, cols), jnp.bfloat16),
        ),
        in_specs=[any_spec, any_spec, any_spec, vmem, vmem, vmem],
        out_specs=(any_spec,) * 4,
        scratch_shapes=[
            pltpu.VMEM((whole, model), jnp.bfloat16),
            pltpu.VMEM((units, model), jnp.bfloat16),
            pltpu.VMEM((n, pairs, width), jnp.bfloat16),
            pltpu.VMEM((whole, units), jnp.bfloat16),
            pltpu.VMEM((whole, pairs), jnp.bfloat16),
            pltpu.VMEM((n, rank, rows), jnp.float32),
            pltpu.VMEM((n, rank, rows), jnp.bfloat16),
            dma((n, count)), dma((n, count)), dma((n, count)), dma((n, count)),
            dma((n,)), dma((n,)), dma((n,)), dma((n,)),
            dma((n,)), dma((n,)), dma((n,)), dma((n,)),
            dma((3,)), dma((n,)), dma((n,)),
        ],
        compiler_params=pltpu.CompilerParams(
            collective_id=0, has_side_effects=True, vmem_limit_bytes=60 * 1024 * 1024
        ),
        cost_estimate=pl.CostEstimate(
            flops=2 * whole * model * (units + pairs), bytes_accessed=4 * whole * model,
            transcendentals=0,
        ),
    )(dy, w, ups, down, ids, part)


def shards(
    output_gradient,
    hidden,
    down_weight_frozen,
    adapter_down_maps,
    adapter_up_maps,
    segment_length_list,
    segment_adapter_index,
    owner_slot_adapter,
    adapter_token_totals,
):
    tok_all, hidden_per_shard = hidden.shape
    rows = output_gradient.shape[0]
    n = tok_all // rows
    width = adapter_up_maps.shape[2]
    count, _, rank = adapter_down_maps.shape
    owner = adapter_table(
        segment_length_list[0], segment_adapter_index[0], tok_all, count
    )
    ids = jnp.sum(
        owner * jnp.arange(count, dtype=jnp.float32)[None, :], axis=1, keepdims=True
    ).astype(jnp.int32)
    hot = (jnp.arange(count * rank, dtype=jnp.int32)[None, :] // rank) == ids
    flat_down = jnp.transpose(adapter_down_maps, (1, 0, 2)).reshape(hidden_per_shard, count * rank)
    flat_up = adapter_up_maps.reshape(count * rank, width)
    down_all = jnp.dot(hidden, flat_down, preferred_element_type=jnp.float32)
    down_part = jnp.sum(
        jnp.where(hot, down_all, 0.0).reshape(tok_all, count, rank), axis=1
    )
    part = jnp.transpose(down_part.reshape(n, rows, rank), (0, 2, 1))
    grad_hidden, up_spread, low_down, cols = gather_and_multiply(
        n, rank, output_gradient, down_weight_frozen, flat_up, flat_down, ids, part
    )
    if cols.shape[1] != width:
        cols = lax.dynamic_slice_in_dim(cols, lax.axis_index("mp") * width, width, 1)
    low_down = jnp.transpose(low_down, (0, 2, 1)).reshape(tok_all, rank)
    down_spread = jnp.where(hot, jnp.tile(low_down, (1, count)), 0).astype(jnp.bfloat16)
    raw_a = 2.0 * lax.dot_general(
        hidden, up_spread, (((0,), (0,)), ((), ())), preferred_element_type=jnp.float32
    )
    raw_b = 2.0 * lax.dot_general(
        down_spread, cols, (((0,), (0,)), ((), ())), preferred_element_type=jnp.float32
    )
    raw_a = jnp.transpose(raw_a.reshape(hidden_per_shard, count, rank), (1, 0, 2))
    raw_b = raw_b.reshape(count, rank, width)
    slot_a = jnp.take(raw_a, owner_slot_adapter, axis=0)
    slot_b = jnp.take(raw_b, owner_slot_adapter, axis=0)
    per_group = count // lax.axis_size("dp")
    first_slot = lax.axis_index("dp") * per_group
    owned_a = lax.psum_scatter(slot_a, "dp", scatter_dimension=0, tiled=True)
    owned_b = lax.psum_scatter(slot_b, "dp", scatter_dimension=0, tiled=True)
    own_slots = lax.dynamic_slice_in_dim(owner_slot_adapter, first_slot, per_group, 0)
    divisor = jnp.take(adapter_token_totals, own_slots, axis=0).astype(jnp.float32)
    grad_a = owned_a / divisor[:, None, None]
    grad_b = owned_b / divisor[:, None, None]
    return (grad_hidden, grad_a, grad_b)


def solution(mesh):
    placed = (
        P(("job", "dp", "mp"), None),
        P(("job", "dp"), "mp"),
        P("mp", None),
        P(None, "mp", None),
        P(None, None, "mp"),
        P(("job", "dp"), None),
        P(("job", "dp"), None),
        P("job"),
        P("job"),
    )
    return jax.shard_map(
        shards,
        mesh=mesh,
        in_specs=placed,
        out_specs=(
            P(("job", "dp"), "mp"),
            P(("job", "dp"), "mp", None),
            P(("job", "dp"), None, "mp"),
        ),
        check_vma=False,
    )
```

```python
import functools

import jax
import jax.numpy as jnp
from jax import lax
from jax.experimental import pallas as pl
from jax.experimental.pallas import tpu as pltpu
from jax.sharding import PartitionSpec as P

MESH = pl.DeviceIdType.MESH
NT = (((1,), (1,)), ((), ()))


def adapter_table(lengths, labels, count_tok, adapter_token_count):
    ends = jnp.cumsum(lengths)
    starts = ends - lengths
    position = jnp.arange(count_tok, dtype=jnp.int32)[:, None]
    inside = ((position >= starts[None, :]) & (position < ends[None, :])).astype(jnp.float32)
    label_hot = (
        labels[:, None] == jnp.arange(adapter_token_count, dtype=jnp.int32)[None, :]
    ).astype(jnp.float32)
    return jnp.dot(inside, label_hot, precision=lax.Precision.HIGHEST)


def chunks_of(rows):
    units = rows // 16
    first = max(1, units * 3 // 16)
    rest = units - first
    parts = min(3, rest)
    sizes = [first] + [rest // parts + (1 if i < rest % parts else 0) for i in range(parts)]
    out, at = [], 0
    for size in sizes:
        out.append((at * 16, size * 16))
        at += size
    return out


def gather_kernel(
    n, jobs, rank,
    dy_ref, w_ref, ups_ref, down_ref, ids_ref, part_ref,
    gh_ref, spread_ref, low_ref, cols_ref,
    g, w_v, u, out_v, spread_v, land, low_v,
    s_up, s_dn, s_y, s_recv, s_us, s_ur, s_ys, s_yr, s_js, s_jr, s_xs, s_xr, s_ps, s_pr, s_ls, s_lr, s_loc, s_out, s_cols,
):
    m = lax.axis_index("mp")
    h = lax.axis_index("dp")
    zs = n // 2
    z, y = m // 2, m % 2
    rows = dy_ref.shape[0]
    half = u.shape[1] // 2
    quarter = half // jobs
    job = lax.axis_index("job")
    other_job = job + 1 - 2 * (job % 2)
    width = u.shape[2]
    units = w_v.shape[0]
    chunks = chunks_of(rows)
    up, dn, across = m + 2, m - 2, z * 2 + (1 - y)

    load_dy = pltpu.make_async_copy(
        dy_ref, g.at[pl.ds(pl.multiple_of(m * rows, 16), rows)], s_loc.at[0]
    )
    load_w = pltpu.make_async_copy(w_ref, w_v, s_loc.at[1])
    load_u = pltpu.make_async_copy(ups_ref, u.at[m], s_loc.at[2])
    load_dy.start()
    load_u.start()
    load_w.start()

    barrier = pltpu.get_barrier_semaphore()
    for k in range(1, n):
        pl.semaphore_signal(barrier, inc=1, device_id={"mp": lax.rem(m + k, n)}, device_id_type=MESH)
    pl.semaphore_signal(barrier, inc=1, device_id={"dp": 1 - h}, device_id_type=MESH)
    if jobs == 2:
        pl.semaphore_signal(barrier, inc=1, device_id={"job": other_job}, device_id_type=MESH)
    pl.semaphore_wait(barrier, n + jobs - 1)

    def block_copy(b, c, sem, to):
        r0, size = chunks[c]
        at = g.at[pl.ds(pl.multiple_of(b * rows + r0, 16), size)]
        return pltpu.make_async_remote_copy(
            src_ref=at, dst_ref=at, send_sem=sem.at[b, c], recv_sem=s_recv.at[b, c],
            device_id={"mp": to}, device_id_type=MESH,
        )

    my_half = pl.ds(pl.multiple_of(h * half, 16), half)
    his_half = pl.ds(pl.multiple_of((1 - h) * half, 16), half)

    def quarter_at(side):
        return pl.ds(pl.multiple_of(h * half + side * quarter, 16), quarter)

    mine = quarter_at(job % 2 if jobs == 2 else 0)
    his = quarter_at(1 - job % 2 if jobs == 2 else 0)

    def origin(k, side):
        return lax.rem(z + zs - k, zs) * 2 + side

    def up_copy(k, b):
        at = u.at[b, mine]
        return pltpu.make_async_remote_copy(
            src_ref=at, dst_ref=at, send_sem=s_us.at[k], recv_sem=s_ur.at[k],
            device_id={"mp": lax.rem(z + k, zs) * 2 + y}, device_id_type=MESH,
        )

    def up_cross(k, b):
        at = u.at[b, mine]
        return pltpu.make_async_remote_copy(
            src_ref=at, dst_ref=at, send_sem=s_ys.at[k], recv_sem=s_yr.at[k],
            device_id={"mp": across}, device_id_type=MESH,
        )

    def up_job(k, part):
        at = u.at[lax.rem(m + n - k, n), part]
        return pltpu.make_async_remote_copy(
            src_ref=at, dst_ref=at, send_sem=s_js.at[k], recv_sem=s_jr.at[k],
            device_id={"job": other_job}, device_id_type=MESH,
        )

    def up_pass(k, part):
        at = u.at[lax.rem(m + n - k, n), part]
        return pltpu.make_async_remote_copy(
            src_ref=at, dst_ref=at, send_sem=s_xs.at[k], recv_sem=s_xr.at[k],
            device_id={"dp": 1 - h}, device_id_type=MESH,
        )

    def part_copy(k):
        to = lax.rem(m + k, n)
        return pltpu.make_async_remote_copy(
            src_ref=part_ref.at[to], dst_ref=land.at[k], send_sem=s_ps.at[k], recv_sem=s_pr.at[k],
            device_id={"mp": to}, device_id_type=MESH,
        )

    def low_copy(k, b):
        to = lax.rem(m + k, n)
        return pltpu.make_async_remote_copy(
            src_ref=low_v.at[b], dst_ref=low_v.at[b], send_sem=s_ls.at[k], recv_sem=s_lr.at[k],
            device_id={"mp": to}, device_id_type=MESH,
        )

    def start_along(b, c, up_too, dn_too):
        @pl.when(up_too)
        def _():
            block_copy(b, c, s_up, up).start()

        @pl.when(dn_too)
        def _():
            block_copy(b, c, s_dn, dn).start()

    can_up, can_dn = z < zs - 1, z > 0
    load_u.wait()
    for k in range(1, zs):
        up_copy(k, m).start()
    up_cross(0, m).start()
    load_dy.wait()
    for c in range(len(chunks)):
        block_copy(m, c, s_y, across).start()
        start_along(m, c, can_up, can_dn)
    for k in range(1, n):
        part_copy(k).start()

    block_copy(across, 0, s_y, across).wait_recv()
    start_along(across, 0, can_up, can_dn)
    for k in range(1, zs):
        up_copy(k, origin(k, y)).wait_recv()
        up_cross(k, origin(k, y)).start()
    for k in range(zs):
        up_cross(k, origin(k, 1 - y)).wait_recv()
    if jobs == 2:
        for k in range(1, n):
            up_job(k, mine).start()
        for k in range(1, n):
            up_job(k, his).wait_recv()
    for k in range(1, n):
        up_pass(k, my_half).start()
    total = part_ref[m]
    for k in range(1, n):
        part_copy(k).wait_recv()
        total = total + land[k]
    low_v[m] = total.astype(jnp.bfloat16)
    for k in range(1, n):
        low_copy(k, m).start()
    for k in range(1, n):
        up_pass(k, his_half).wait_recv()
    load_w.wait()

    def cols_copy(b):
        r = pl.ds(pl.multiple_of(b * rows, 16), rows)
        if cols_ref.shape[1] == g.shape[1]:
            return pltpu.make_async_copy(g.at[r], cols_ref.at[r], s_cols.at[b])
        c = pl.ds(pl.multiple_of(m * width, 128), width)
        return pltpu.make_async_copy(g.at[r, c], cols_ref.at[r], s_cols.at[b])

    def out_copy(b):
        r = pl.ds(pl.multiple_of(b * rows, 16), rows)
        return pltpu.make_async_copy(out_v.at[r], gh_ref.at[r], s_out.at[b])

    tile = 512
    edges = [(i, min(tile, units - i)) for i in range(0, units, tile)]

    def compute(b):
        r = pl.ds(pl.multiple_of(b * rows, 16), rows)
        cols_copy(b).start()
        val = jnp.zeros((rows, 2 * half), jnp.float32)
        for j in range(n):
            val = val + lax.dot_general(
                g[r, j * width:(j + 1) * width], u[j], NT, preferred_element_type=jnp.float32
            )
        lane = lax.broadcasted_iota(jnp.int32, (rows, 2 * half), 1) // rank
        low = jnp.where(lane == ids_ref[r], val, 0.0).astype(jnp.bfloat16)
        spread_v[r] = low
        for c0, size in edges:
            acc = lax.dot_general(
                g[r], w_v[c0:c0 + size], NT, preferred_element_type=jnp.float32
            )
            acc = acc + 2.0 * lax.dot_general(
                low, down_ref[c0:c0 + size], NT, preferred_element_type=jnp.float32
            )
            out_v[r, c0:c0 + size] = acc.astype(jnp.bfloat16)
        out_copy(b).start()

    def step(d, carry):
        lo, hi = z - d, z + d
        moving = d > 0
        lo_in, hi_in = moving & (lo >= 0), moving & (hi < zs)

        def pass_on(c, side, crosses):
            @pl.when(lo_in)
            def _():
                b = lo * 2 + side
                block_copy(b, c, s_up, across).wait_recv()
                if crosses:
                    block_copy(b, c, s_y, across).start()

                @pl.when(can_up)
                def _():
                    block_copy(b, c, s_up, up).start()

            @pl.when(hi_in)
            def _():
                b = hi * 2 + side
                block_copy(b, c, s_dn, across).wait_recv()
                if crosses:
                    block_copy(b, c, s_y, across).start()

                @pl.when(can_dn)
                def _():
                    block_copy(b, c, s_dn, dn).start()

        def pair(dist, own):
            def one(i, carry):
                zz = jnp.where(i == 0, z - dist, z + dist)
                ok = (dist >= 0) & (zz >= 0) & (zz < zs) & ((i == 0) | (dist > 0))
                b = zz * 2 + (y if own else 1 - y)

                @pl.when(ok)
                def _():
                    if not own:
                        for c in range(1, len(chunks)):
                            block_copy(b, c, s_y, across).wait_recv()
                    compute(b)
                return carry

            lax.fori_loop(0, 2, one, 0)

        for c in range(1, len(chunks) - 1):
            pass_on(c, y, True)
        pass_on(len(chunks) - 1, y, True)
        pair(d - 1, False)
        pass_on(0, y, False)
        pass_on(0, 1 - y, False)
        pair(d, True)
        return carry

    lax.fori_loop(0, zs + 1, step, 0)

    for k in range(1, n):
        low_copy(k, lax.rem(m + n - k, n)).wait_recv()
    low_out = pltpu.make_async_copy(low_v, low_ref, s_loc.at[0])
    spread_out = pltpu.make_async_copy(spread_v, spread_ref, s_loc.at[1])
    low_out.start()
    spread_out.start()

    for k in range(1, n):
        if k < zs:
            up_copy(k, m).wait_send()
        if jobs == 2:
            up_job(k, mine).wait_send()
        up_pass(k, my_half).wait_send()
        part_copy(k).wait_send()
        low_copy(k, m).wait_send()

    for k in range(zs):
        up_cross(k, origin(k, y)).wait_send()

    def drain(b, carry):
        bz, by = b // 2, b % 2
        for c in range(len(chunks)):
            zway = (by == y) if c else (bz >= 0)

            @pl.when(can_up & (bz <= z) & zway)
            def _():
                block_copy(b, c, s_up, up).wait_send()

            @pl.when(can_dn & (bz >= z) & zway)
            def _():
                block_copy(b, c, s_dn, dn).wait_send()

            @pl.when((by == y) & (True if c else (bz == z)))
            def _():
                block_copy(b, c, s_y, across).wait_send()
        cols_copy(b).wait()
        out_copy(b).wait()
        return carry

    lax.fori_loop(0, n, drain, 0)
    low_out.wait()
    spread_out.wait()


def gather_and_multiply(n, jobs, rank, dy, w, ups, down, ids, part):
    rows, model = dy.shape
    units = w.shape[0]
    pairs, width = ups.shape
    whole = n * rows
    cols = width if width % 128 == 0 else model
    count = len(chunks_of(rows))
    any_spec = pl.BlockSpec(memory_space=pl.ANY)
    vmem = pl.BlockSpec(memory_space=pltpu.VMEM)
    dma = pltpu.SemaphoreType.DMA
    return pl.pallas_call(
        functools.partial(gather_kernel, n, jobs, rank),
        out_shape=(
            jax.ShapeDtypeStruct((whole, units), jnp.bfloat16),
            jax.ShapeDtypeStruct((whole, pairs), jnp.bfloat16),
            jax.ShapeDtypeStruct((n, rank, rows), jnp.bfloat16),
            jax.ShapeDtypeStruct((whole, cols), jnp.bfloat16),
        ),
        in_specs=[any_spec, any_spec, any_spec, vmem, vmem, vmem],
        out_specs=(any_spec,) * 4,
        scratch_shapes=[
            pltpu.VMEM((whole, model), jnp.bfloat16),
            pltpu.VMEM((units, model), jnp.bfloat16),
            pltpu.VMEM((n, pairs, width), jnp.bfloat16),
            pltpu.VMEM((whole, units), jnp.bfloat16),
            pltpu.VMEM((whole, pairs), jnp.bfloat16),
            pltpu.VMEM((n, rank, rows), jnp.float32),
            pltpu.VMEM((n, rank, rows), jnp.bfloat16),
            dma((n, count)), dma((n, count)), dma((n, count)), dma((n, count)),
            dma((n,)), dma((n,)), dma((n,)), dma((n,)),
            dma((n,)), dma((n,)), dma((n,)), dma((n,)),
            dma((n,)), dma((n,)), dma((n,)), dma((n,)),
            dma((3,)), dma((n,)), dma((n,)),
        ],
        compiler_params=pltpu.CompilerParams(
            collective_id=0, has_side_effects=True, vmem_limit_bytes=60 * 1024 * 1024
        ),
        cost_estimate=pl.CostEstimate(
            flops=2 * whole * model * (units + pairs), bytes_accessed=4 * whole * model,
            transcendentals=0,
        ),
    )(dy, w, ups, down, ids, part)


def shards(
    output_gradient,
    hidden,
    down_weight_frozen,
    adapter_down_maps,
    adapter_up_maps,
    segment_length_list,
    segment_adapter_index,
    owner_slot_adapter,
    adapter_token_totals,
):
    tok_all, hidden_per_shard = hidden.shape
    rows = output_gradient.shape[0]
    n = tok_all // rows
    width = adapter_up_maps.shape[2]
    count, _, rank = adapter_down_maps.shape
    owner = adapter_table(
        segment_length_list[0], segment_adapter_index[0], tok_all, count
    )
    ids = jnp.sum(
        owner * jnp.arange(count, dtype=jnp.float32)[None, :], axis=1, keepdims=True
    ).astype(jnp.int32)
    hot = (jnp.arange(count * rank, dtype=jnp.int32)[None, :] // rank) == ids
    flat_down = jnp.transpose(adapter_down_maps, (1, 0, 2)).reshape(hidden_per_shard, count * rank)
    flat_up = adapter_up_maps.reshape(count * rank, width)
    down_all = jnp.dot(hidden, flat_down, preferred_element_type=jnp.float32)
    down_part = jnp.sum(
        jnp.where(hot, down_all, 0.0).reshape(tok_all, count, rank), axis=1
    )
    part = jnp.transpose(down_part.reshape(n, rows, rank), (0, 2, 1))
    grad_hidden, up_spread, low_down, cols = gather_and_multiply(
        n, 2 if lax.axis_size("job") % 2 == 0 else 1, rank, output_gradient, down_weight_frozen, flat_up, flat_down, ids, part
    )
    if cols.shape[1] != width:
        cols = lax.dynamic_slice_in_dim(cols, lax.axis_index("mp") * width, width, 1)
    low_down = jnp.transpose(low_down, (0, 2, 1)).reshape(tok_all, rank)
    down_spread = jnp.where(hot, jnp.tile(low_down, (1, count)), 0).astype(jnp.bfloat16)
    raw_a = 2.0 * lax.dot_general(
        hidden, up_spread, (((0,), (0,)), ((), ())), preferred_element_type=jnp.float32
    )
    raw_b = 2.0 * lax.dot_general(
        down_spread, cols, (((0,), (0,)), ((), ())), preferred_element_type=jnp.float32
    )
    raw_a = jnp.transpose(raw_a.reshape(hidden_per_shard, count, rank), (1, 0, 2))
    raw_b = raw_b.reshape(count, rank, width)
    slot_a = jnp.take(raw_a, owner_slot_adapter, axis=0)
    slot_b = jnp.take(raw_b, owner_slot_adapter, axis=0)
    per_group = count // lax.axis_size("dp")
    first_slot = lax.axis_index("dp") * per_group
    owned_a = lax.psum_scatter(slot_a, "dp", scatter_dimension=0, tiled=True)
    owned_b = lax.psum_scatter(slot_b, "dp", scatter_dimension=0, tiled=True)
    own_slots = lax.dynamic_slice_in_dim(owner_slot_adapter, first_slot, per_group, 0)
    divisor = jnp.take(adapter_token_totals, own_slots, axis=0).astype(jnp.float32)
    grad_a = owned_a / divisor[:, None, None]
    grad_b = owned_b / divisor[:, None, None]
    return (grad_hidden, grad_a, grad_b)


def solution(mesh):
    placed = (
        P(("job", "dp", "mp"), None),
        P(("job", "dp"), "mp"),
        P("mp", None),
        P(None, "mp", None),
        P(None, None, "mp"),
        P(("job", "dp"), None),
        P(("job", "dp"), None),
        P("job"),
        P("job"),
    )
    return jax.shard_map(
        shards,
        mesh=mesh,
        in_specs=placed,
        out_specs=(
            P(("job", "dp"), "mp"),
            P(("job", "dp"), "mp", None),
            P(("job", "dp"), None, "mp"),
        ),
        check_vma=False,
    )
```

```python
import functools

import jax
import jax.numpy as jnp
from jax import lax
from jax.experimental import pallas as pl
from jax.experimental.pallas import tpu as pltpu
from jax.sharding import PartitionSpec as P

MESH = pl.DeviceIdType.MESH
NT = (((1,), (1,)), ((), ()))


def adapter_table(lengths, labels, count_tok, adapter_token_count):
    ends = jnp.cumsum(lengths)
    starts = ends - lengths
    position = jnp.arange(count_tok, dtype=jnp.int32)[:, None]
    inside = ((position >= starts[None, :]) & (position < ends[None, :])).astype(jnp.float32)
    label_hot = (
        labels[:, None] == jnp.arange(adapter_token_count, dtype=jnp.int32)[None, :]
    ).astype(jnp.float32)
    return jnp.dot(inside, label_hot, precision=lax.Precision.HIGHEST)


def chunks_of(rows):
    units = rows // 16
    first = max(1, units * 3 // 16)
    rest = units - first
    parts = min(3, rest)
    sizes = [first] + [rest // parts + (1 if i < rest % parts else 0) for i in range(parts)]
    out, at = [], 0
    for size in sizes:
        out.append((at * 16, size * 16))
        at += size
    return out


def gather_kernel(
    n, jobs, rank,
    dy_ref, w_ref, ups_ref, down_ref, ids_ref, part_ref,
    gh_ref, spread_ref, low_ref, cols_ref,
    g, w_v, u, out_v, spread_v, land, low_v,
    s_up, s_dn, s_y, s_recv, s_us, s_ur, s_ys, s_yr, s_js, s_jr, s_xs, s_xr, s_ps, s_pr, s_ls, s_lr, s_loc, s_out, s_cols,
):
    m = lax.axis_index("mp")
    h = lax.axis_index("dp")
    zs = n // 2
    z, y = m // 2, m % 2
    rows = dy_ref.shape[0]
    half = u.shape[1] // 2
    quarter = half // jobs
    job = lax.axis_index("job")
    other_job = job + 1 - 2 * (job % 2)
    width = u.shape[2]
    units = w_v.shape[0]
    chunks = chunks_of(rows)
    up, dn, across = m + 2, m - 2, z * 2 + (1 - y)

    load_dy = pltpu.make_async_copy(
        dy_ref, g.at[pl.ds(pl.multiple_of(m * rows, 16), rows)], s_loc.at[0]
    )
    load_w = pltpu.make_async_copy(w_ref, w_v, s_loc.at[1])
    load_u = pltpu.make_async_copy(ups_ref, u.at[m], s_loc.at[2])
    load_dy.start()
    load_u.start()
    load_w.start()

    barrier = pltpu.get_barrier_semaphore()
    for k in range(1, n):
        pl.semaphore_signal(barrier, inc=1, device_id={"mp": lax.rem(m + k, n)}, device_id_type=MESH)
    pl.semaphore_signal(barrier, inc=1, device_id={"dp": 1 - h}, device_id_type=MESH)
    if jobs == 2:
        pl.semaphore_signal(barrier, inc=1, device_id={"job": other_job}, device_id_type=MESH)
    pl.semaphore_wait(barrier, n + jobs - 1)

    def block_copy(b, c, sem, to):
        r0, size = chunks[c]
        at = g.at[pl.ds(pl.multiple_of(b * rows + r0, 16), size)]
        return pltpu.make_async_remote_copy(
            src_ref=at, dst_ref=at, send_sem=sem.at[b, c], recv_sem=s_recv.at[b, c],
            device_id={"mp": to}, device_id_type=MESH,
        )

    my_half = pl.ds(pl.multiple_of(h * half, 16), half)
    his_half = pl.ds(pl.multiple_of((1 - h) * half, 16), half)

    def quarter_at(side):
        return pl.ds(pl.multiple_of(h * half + side * quarter, 16), quarter)

    mine = quarter_at(job % 2 if jobs == 2 else 0)
    his = quarter_at(1 - job % 2 if jobs == 2 else 0)

    def origin(k, side):
        return lax.rem(z + zs - k, zs) * 2 + side

    def up_copy(k, b):
        at = u.at[b, mine]
        return pltpu.make_async_remote_copy(
            src_ref=at, dst_ref=at, send_sem=s_us.at[k], recv_sem=s_ur.at[k],
            device_id={"mp": lax.rem(z + k, zs) * 2 + y}, device_id_type=MESH,
        )

    def up_cross(k, b):
        at = u.at[b, mine]
        return pltpu.make_async_remote_copy(
            src_ref=at, dst_ref=at, send_sem=s_ys.at[k], recv_sem=s_yr.at[k],
            device_id={"mp": across}, device_id_type=MESH,
        )

    def up_job(k, part):
        at = u.at[lax.rem(m + n - k, n), part]
        return pltpu.make_async_remote_copy(
            src_ref=at, dst_ref=at, send_sem=s_js.at[k], recv_sem=s_jr.at[k],
            device_id={"job": other_job}, device_id_type=MESH,
        )

    def up_pass(k, part):
        at = u.at[lax.rem(m + n - k, n), part]
        return pltpu.make_async_remote_copy(
            src_ref=at, dst_ref=at, send_sem=s_xs.at[k], recv_sem=s_xr.at[k],
            device_id={"dp": 1 - h}, device_id_type=MESH,
        )

    def part_copy(k):
        to = lax.rem(m + k, n)
        return pltpu.make_async_remote_copy(
            src_ref=part_ref.at[to], dst_ref=land.at[k], send_sem=s_ps.at[k], recv_sem=s_pr.at[k],
            device_id={"mp": to}, device_id_type=MESH,
        )

    def low_copy(k, b):
        to = lax.rem(m + k, n)
        return pltpu.make_async_remote_copy(
            src_ref=low_v.at[b], dst_ref=low_v.at[b], send_sem=s_ls.at[k], recv_sem=s_lr.at[k],
            device_id={"mp": to}, device_id_type=MESH,
        )

    def start_along(b, c, up_too, dn_too):
        @pl.when(up_too)
        def _():
            block_copy(b, c, s_up, up).start()

        @pl.when(dn_too)
        def _():
            block_copy(b, c, s_dn, dn).start()

    can_up, can_dn = z < zs - 1, z > 0
    load_u.wait()
    for k in range(1, zs):
        up_copy(k, m).start()
    up_cross(0, m).start()
    load_dy.wait()
    for c in range(len(chunks)):
        block_copy(m, c, s_y, across).start()
        start_along(m, c, can_up, can_dn)
    for k in range(1, n):
        part_copy(k).start()

    block_copy(across, 0, s_y, across).wait_recv()
    start_along(across, 0, can_up, can_dn)
    for k in range(1, zs):
        up_copy(k, origin(k, y)).wait_recv()
        up_cross(k, origin(k, y)).start()
    for k in range(zs):
        up_cross(k, origin(k, 1 - y)).wait_recv()
    if jobs == 2:
        for k in range(1, n):
            up_job(k, mine).start()
        for k in range(1, n):
            up_job(k, his).wait_recv()
    for k in range(1, n):
        up_pass(k, my_half).start()
    total = part_ref[m]
    for k in range(1, n):
        part_copy(k).wait_recv()
        total = total + land[k]
    low_v[m] = total.astype(jnp.bfloat16)
    for k in range(1, n):
        low_copy(k, m).start()
    for k in range(1, n):
        up_pass(k, his_half).wait_recv()
    load_w.wait()

    def cols_copy(b):
        r = pl.ds(pl.multiple_of(b * rows, 16), rows)
        if cols_ref.shape[1] == g.shape[1]:
            return pltpu.make_async_copy(g.at[r], cols_ref.at[r], s_cols.at[b])
        c = pl.ds(pl.multiple_of(m * width, 128), width)
        return pltpu.make_async_copy(g.at[r, c], cols_ref.at[r], s_cols.at[b])

    def out_copy(b):
        r = pl.ds(pl.multiple_of(b * rows, 16), rows)
        return pltpu.make_async_copy(out_v.at[r], gh_ref.at[r], s_out.at[b])

    tile = 512
    edges = [(i, min(tile, units - i)) for i in range(0, units, tile)]

    def compute(b):
        r = pl.ds(pl.multiple_of(b * rows, 16), rows)
        cols_copy(b).start()
        val = jnp.zeros((rows, 2 * half), jnp.float32)
        for j in range(n):
            val = val + lax.dot_general(
                g[r, j * width:(j + 1) * width], u[j], NT, preferred_element_type=jnp.float32
            )
        lane = lax.broadcasted_iota(jnp.int32, (rows, 2 * half), 1) // rank
        low = jnp.where(lane == ids_ref[r], val, 0.0).astype(jnp.bfloat16)
        spread_v[r] = low
        for c0, size in edges:
            acc = lax.dot_general(
                g[r], w_v[c0:c0 + size], NT, preferred_element_type=jnp.float32
            )
            acc = acc + 2.0 * lax.dot_general(
                low, down_ref[c0:c0 + size], NT, preferred_element_type=jnp.float32
            )
            out_v[r, c0:c0 + size] = acc.astype(jnp.bfloat16)
        out_copy(b).start()

    def step(d, carry):
        lo, hi = z - d, z + d
        moving = d > 0
        lo_in, hi_in = moving & (lo >= 0), moving & (hi < zs)

        def pass_on(c, side, crosses):
            @pl.when(lo_in)
            def _():
                b = lo * 2 + side
                block_copy(b, c, s_up, across).wait_recv()
                if crosses:
                    block_copy(b, c, s_y, across).start()

                @pl.when(can_up)
                def _():
                    block_copy(b, c, s_up, up).start()

            @pl.when(hi_in)
            def _():
                b = hi * 2 + side
                block_copy(b, c, s_dn, across).wait_recv()
                if crosses:
                    block_copy(b, c, s_y, across).start()

                @pl.when(can_dn)
                def _():
                    block_copy(b, c, s_dn, dn).start()

        def pair(dist, own):
            def one(i, carry):
                zz = jnp.where(i == 0, z - dist, z + dist)
                ok = (dist >= 0) & (zz >= 0) & (zz < zs) & ((i == 0) | (dist > 0))
                b = zz * 2 + (y if own else 1 - y)

                @pl.when(ok)
                def _():
                    if not own:
                        for c in range(1, len(chunks)):
                            block_copy(b, c, s_y, across).wait_recv()
                    compute(b)
                return carry

            lax.fori_loop(0, 2, one, 0)

        for c in range(1, len(chunks) - 1):
            pass_on(c, y, True)
        pass_on(len(chunks) - 1, y, True)
        pair(d - 1, False)
        pass_on(0, y, False)
        pass_on(0, 1 - y, False)
        pair(d, True)
        return carry

    lax.fori_loop(0, zs + 1, step, 0)

    for k in range(1, n):
        low_copy(k, lax.rem(m + n - k, n)).wait_recv()
    low_out = pltpu.make_async_copy(low_v, low_ref, s_loc.at[0])
    spread_out = pltpu.make_async_copy(spread_v, spread_ref, s_loc.at[1])
    low_out.start()
    spread_out.start()

    for k in range(1, n):
        if k < zs:
            up_copy(k, m).wait_send()
        if jobs == 2:
            up_job(k, mine).wait_send()
        up_pass(k, my_half).wait_send()
        part_copy(k).wait_send()
        low_copy(k, m).wait_send()

    for k in range(zs):
        up_cross(k, origin(k, y)).wait_send()

    def drain(b, carry):
        bz, by = b // 2, b % 2
        for c in range(len(chunks)):
            zway = (by == y) if c else (bz >= 0)

            @pl.when(can_up & (bz <= z) & zway)
            def _():
                block_copy(b, c, s_up, up).wait_send()

            @pl.when(can_dn & (bz >= z) & zway)
            def _():
                block_copy(b, c, s_dn, dn).wait_send()

            @pl.when((by == y) & (True if c else (bz == z)))
            def _():
                block_copy(b, c, s_y, across).wait_send()
        cols_copy(b).wait()
        out_copy(b).wait()
        return carry

    lax.fori_loop(0, n, drain, 0)
    low_out.wait()
    spread_out.wait()


def gather_and_multiply(n, jobs, rank, dy, w, ups, down, ids, part):
    rows, model = dy.shape
    units = w.shape[0]
    pairs, width = ups.shape
    whole = n * rows
    cols = width if width % 128 == 0 else model
    count = len(chunks_of(rows))
    any_spec = pl.BlockSpec(memory_space=pl.ANY)
    vmem = pl.BlockSpec(memory_space=pltpu.VMEM)
    dma = pltpu.SemaphoreType.DMA
    return pl.pallas_call(
        functools.partial(gather_kernel, n, jobs, rank),
        out_shape=(
            jax.ShapeDtypeStruct((whole, units), jnp.bfloat16),
            jax.ShapeDtypeStruct((whole, pairs), jnp.bfloat16),
            jax.ShapeDtypeStruct((n, rank, rows), jnp.bfloat16),
            jax.ShapeDtypeStruct((whole, cols), jnp.bfloat16),
        ),
        in_specs=[any_spec, any_spec, any_spec, vmem, vmem, vmem],
        out_specs=(any_spec,) * 4,
        scratch_shapes=[
            pltpu.VMEM((whole, model), jnp.bfloat16),
            pltpu.VMEM((units, model), jnp.bfloat16),
            pltpu.VMEM((n, pairs, width), jnp.bfloat16),
            pltpu.VMEM((whole, units), jnp.bfloat16),
            pltpu.VMEM((whole, pairs), jnp.bfloat16),
            pltpu.VMEM((n, rank, rows), jnp.float32),
            pltpu.VMEM((n, rank, rows), jnp.bfloat16),
            dma((n, count)), dma((n, count)), dma((n, count)), dma((n, count)),
            dma((n,)), dma((n,)), dma((n,)), dma((n,)),
            dma((n,)), dma((n,)), dma((n,)), dma((n,)),
            dma((n,)), dma((n,)), dma((n,)), dma((n,)),
            dma((3,)), dma((n,)), dma((n,)),
        ],
        compiler_params=pltpu.CompilerParams(
            collective_id=0, has_side_effects=True, vmem_limit_bytes=60 * 1024 * 1024
        ),
        cost_estimate=pl.CostEstimate(
            flops=2 * whole * model * (units + pairs), bytes_accessed=4 * whole * model,
            transcendentals=0,
        ),
    )(dy, w, ups, down, ids, part)


def shards(
    output_gradient,
    hidden,
    down_weight_frozen,
    adapter_down_maps,
    adapter_up_maps,
    segment_length_list,
    segment_adapter_index,
    owner_slot_adapter,
    adapter_token_totals,
):
    tok_all, hidden_per_shard = hidden.shape
    rows = output_gradient.shape[0]
    n = tok_all // rows
    width = adapter_up_maps.shape[2]
    count, _, rank = adapter_down_maps.shape
    owner = adapter_table(
        segment_length_list[0], segment_adapter_index[0], tok_all, count
    )
    ids = jnp.sum(
        owner * jnp.arange(count, dtype=jnp.float32)[None, :], axis=1, keepdims=True
    ).astype(jnp.int32)
    hot = (jnp.arange(count * rank, dtype=jnp.int32)[None, :] // rank) == ids
    flat_down = jnp.transpose(adapter_down_maps, (1, 0, 2)).reshape(hidden_per_shard, count * rank)
    flat_up = adapter_up_maps.reshape(count * rank, width)
    down_all = jnp.dot(hidden, flat_down, preferred_element_type=jnp.float32)
    down_part = jnp.sum(
        jnp.where(hot, down_all, 0.0).reshape(tok_all, count, rank), axis=1
    )
    part = jnp.transpose(down_part.reshape(n, rows, rank), (0, 2, 1))
    grad_hidden, up_spread, low_down, cols = gather_and_multiply(
        n, 2 if lax.axis_size("job") % 2 == 0 else 1, rank, output_gradient, down_weight_frozen, flat_up, flat_down, ids, part
    )
    if cols.shape[1] != width:
        cols = lax.dynamic_slice_in_dim(cols, lax.axis_index("mp") * width, width, 1)
    low_down = jnp.transpose(low_down, (0, 2, 1)).reshape(tok_all, rank)
    lanes = jnp.arange(count * rank, dtype=jnp.int32)
    source = jnp.repeat(owner_slot_adapter, rank) * rank + lanes % rank
    order = (lanes[:, None] == source[None, :]).astype(jnp.bfloat16)
    up_spread = jnp.dot(up_spread, order, preferred_element_type=jnp.float32).astype(jnp.bfloat16)
    hot_slot = ids == (source // rank)[None, :]
    down_spread = jnp.where(hot_slot, jnp.tile(low_down, (1, count)), 0).astype(jnp.bfloat16)
    raw_a = 2.0 * lax.dot_general(
        hidden, up_spread, (((0,), (0,)), ((), ())), preferred_element_type=jnp.float32
    )
    raw_b = 2.0 * lax.dot_general(
        down_spread, cols, (((0,), (0,)), ((), ())), preferred_element_type=jnp.float32
    )
    raw_a = jnp.transpose(raw_a.reshape(hidden_per_shard, count, rank), (1, 0, 2))
    raw_b = raw_b.reshape(count, rank, width)
    per_group = count // lax.axis_size("dp")
    first_slot = lax.axis_index("dp") * per_group
    owned_a = lax.psum_scatter(raw_a, "dp", scatter_dimension=0, tiled=True)
    owned_b = lax.psum_scatter(raw_b, "dp", scatter_dimension=0, tiled=True)
    own_slots = lax.dynamic_slice_in_dim(owner_slot_adapter, first_slot, per_group, 0)
    divisor = jnp.take(adapter_token_totals, own_slots, axis=0).astype(jnp.float32)
    grad_a = owned_a / divisor[:, None, None]
    grad_b = owned_b / divisor[:, None, None]
    return (grad_hidden, grad_a, grad_b)


def solution(mesh):
    placed = (
        P(("job", "dp", "mp"), None),
        P(("job", "dp"), "mp"),
        P("mp", None),
        P(None, "mp", None),
        P(None, None, "mp"),
        P(("job", "dp"), None),
        P(("job", "dp"), None),
        P("job"),
        P("job"),
    )
    return jax.shard_map(
        shards,
        mesh=mesh,
        in_specs=placed,
        out_specs=(
            P(("job", "dp"), "mp"),
            P(("job", "dp"), "mp", None),
            P(("job", "dp"), None, "mp"),
        ),
        check_vma=False,
    )
```
